32 devices in a mesh: grp: 2 (over x), row: 16 (over z, y, core).
Axes of the slice: x: 2, y: 2, z: 4, core: 2. Of those that a mesh axis runs over, the one named last changes fastest.
Arguments:
- amps: float32 [1024, 4096], P(('grp', 'row')), parts along dimension 0, may hold values from -6 to 6
- amp_mask: int32 [256, 16], P('grp'), parts along dimension 0, may hold values 0 or 1
- integrals: float32 [256, 256, 256], P(('grp', 'row')), parts along dimension 0, may hold values from -0.09375 to 0.09375
- slot_tile: int32 [256], P('grp'), parts along dimension 0, may hold values from 0 to 127, each once
- int_mask: int32 [256], P('grp'), parts along dimension 0, may hold values 0 or 1
Outputs:
- ladder: float32 [1024, 2048], P(('grp', 'row')), parts along dimension 0
The draws below stay inside these ranges and needn't reach their ends.
There are 2 independent parts, one for each index of `grp`. The reference program is written for one: setup_inputs(seed, part) draws one part's arguments, and reference() takes and returns one part's arrays. A program takes and returns all parts, laid end to end along the dimension named above; each array names one. Nothing has to cross between parts.
All inputs are finite; a program needn't handle non-finite values.
Results may differ from the reference program's by a relative error of at most 0.000071.
Values sent between devices are 32-bit elements; how exact they have to be, the bound alone decides.
A program may use at most 64 MiB of HBM per device.

```python
import jax
import jax.numpy as jnp
from jax import lax

NV = 2048
TILE = 256
PANELS = 2
PTILE = 4
NT = 8
P_SIZE = 512
NTILES = 128


def touch_ends(entries, rng, low, top_value):
    shape = entries.shape
    spot = [jax.random.randint(jax.random.fold_in(rng, axis), (), 0, shape[axis]) for axis in range(len(shape))]
    entries = entries.at[tuple(spot)].set(low)
    longest = shape.index(max(shape))
    spot[longest] = (spot[longest] + 1) % shape[longest]
    return entries.at[tuple(spot)].set(top_value)


def steps_of(own_key, dims, shards, smallest, high):
    level = 1.0
    for axis_at, shards_of in shards:
        heights = jax.random.uniform(jax.random.fold_in(jax.random.fold_in(own_key, 6), axis_at), (shards_of,), jnp.float32, smallest / len(shards), high / len(shards))
        level = level * jnp.repeat(jnp.exp(heights), dims[axis_at] // shards_of).reshape((-1,) + (1,) * (len(dims) - 1 - axis_at))
    return level


def normal_values(key, shape, width, limit, split=(), held_as=jnp.bfloat16):
    gain = steps_of(key, shape, split, -0.22, 0.18) if split else 1.0
    drawn = jax.random.normal(key, shape, jnp.float32) * width * gain
    return jnp.minimum(jnp.maximum(drawn, -limit), limit).astype(held_as)


def setup_inputs(seed: int = 0, part: int = 0) -> dict:
    seeds = jax.random.split(jax.random.key(seed), 6)
    part_keys = jax.random.split(jax.random.fold_in(seeds[5], part), 6)
    amps = normal_values(part_keys[0], (P_SIZE, PANELS * NV), 1.0, 6.0, ((0, 16),), jnp.float32)
    amp_mask = touch_ends((jax.random.randint(part_keys[1], (P_SIZE // PTILE, PANELS * NT), 0, 3) < 1).astype(jnp.int32), jax.random.fold_in(part_keys[1], 1), 0, 1)
    integrals = normal_values(part_keys[2], (NTILES, TILE, TILE), (PANELS * NV) ** -0.5, 0.09375, ((0, 16),), jnp.float32)
    slot_tile = jax.random.permutation(part_keys[3], NTILES).astype(jnp.int32)
    int_mask = touch_ends((jax.random.randint(part_keys[4], (NTILES,), 0, 3) < 1).astype(jnp.int32), jax.random.fold_in(part_keys[4], 1), 0, 1)
    return dict(amps=amps, amp_mask=amp_mask, integrals=integrals, slot_tile=slot_tile, int_mask=int_mask)


def reference(amps, amp_mask, integrals, slot_tile, int_mask):
    by_tile = jnp.zeros_like(integrals).at[slot_tile].set(integrals)
    by_tile = by_tile * int_mask.astype(jnp.float32)[:, None, None]
    weights = by_tile.reshape(PANELS, NT, NT, TILE, TILE).transpose(0, 1, 3, 2, 4).reshape(PANELS * NV, NV)
    rows_mask = jnp.repeat(jnp.repeat(amp_mask.astype(jnp.float32), PTILE, axis=0), TILE, axis=1)
    masked = amps * rows_mask
    return jnp.dot(masked, weights, precision=lax.Precision.HIGHEST, preferred_element_type=jnp.float32)
```

```python
import functools

import jax
import jax.numpy as jnp
from jax import lax
from jax.experimental import pallas as pl
from jax.experimental.pallas import tpu as pltpu
from jax.sharding import PartitionSpec as P

PTILE = 4
MESH = pl.DeviceIdType.MESH
F32 = jnp.float32
BF16 = jnp.bfloat16


def kernel(
    n, snake, nt, amps, amp_mask, integ, meta, out,
    ag, wsib, wcat, aw, prod, part, rs, fin,
    ag_recv, ag_right, ag_left, ag_sib, rs_recv, rs_send, w_sems, fin_sems,
):
    rows, width = amps.shape
    slots, tile, _ = integ.shape
    half = tile // 2
    blocks = width // tile
    hr = rows // 2
    far = n // 2
    grp = lax.axis_index("grp")
    r = lax.axis_index("row")
    chip, core = r // 2, r % 2
    other = 1 - core

    if snake:
        z, y, length = chip // 2, chip % 2, n // 2
        pos = (1 - y) * z + y * (n - 1 - z)

        def chip_at(q):
            up = q // length
            return (1 - up) * (2 * q) + up * (2 * (n - 1 - q) + 1)
    else:
        pos = chip

        def chip_at(q):
            return q

    right = (grp, chip_at((pos + 1) % n) * 2 + core)
    left = (grp, chip_at((pos + n - 1) % n) * 2 + core)
    sib_row = chip * 2 + other
    sibling = (grp, sib_row)

    barrier = pltpu.get_barrier_semaphore()
    for who in (right, left, sibling):
        pl.semaphore_signal(barrier, inc=1, device_id=who, device_id_type=MESH)

    def mine(k, c):
        return ag.at[k, c, pl.ds(pl.multiple_of(core * hr, hr), hr), :]

    mrows = rows // PTILE
    m8 = amp_mask[pl.ds(pl.multiple_of(r * mrows, mrows), mrows), :].astype(F32)
    pick = (
        lax.broadcasted_iota(jnp.int32, (rows, mrows), 0) // PTILE
        == lax.broadcasted_iota(jnp.int32, (rows, mrows), 1)
    ).astype(F32)
    mask = jnp.dot(pick, m8, preferred_element_type=F32)
    for j in range(blocks):
        seg = amps[:, j * tile:(j + 1) * tile] * mask[:, j:j + 1]
        for c in range(2):
            ag[0, c, pl.ds(pl.multiple_of(core * hr, hr), hr), j * tile:(j + 1) * tile] = (
                seg[c * hr:(c + 1) * hr]
            )

    pl.semaphore_wait(barrier, 3)

    pending = []

    def send(src, dst, ssem, rsem, who):
        cp = pltpu.make_async_remote_copy(
            src_ref=src, dst_ref=dst, send_sem=ssem, recv_sem=rsem,
            device_id=who, device_id_type=MESH,
        )
        cp.start()
        pending.append(cp)

    def got(dst, rsem, ssem, who):
        pltpu.make_async_remote_copy(
            src_ref=dst, dst_ref=dst, send_sem=ssem, recv_sem=rsem,
            device_id=who, device_id_type=MESH,
        ).wait_recv()

    def go_right(k, c):
        send(mine(k, c), mine(k + 1, c), ag_right.at[k, c], ag_recv.at[k + 1, c, 0], right)

    def go_left(k, c):
        k0 = k if k else n
        send(mine(k, c), mine(k0 - 1, c), ag_left.at[k, c], ag_recv.at[k0 - 1, c, 0], left)

    def go_sib(k, c):
        send(mine(k, c), mine(k, c), ag_sib.at[k, c], ag_recv.at[k, c, 1], sibling)

    def from_ring(k, c):
        got(mine(k, c), ag_recv.at[k, c, 0], ag_sib.at[k, c], sibling)

    def from_sib(k, c):
        theirs = ag.at[k, c, pl.ds(pl.multiple_of(other * hr, hr), hr), :]
        got(theirs, ag_recv.at[k, c, 1], ag_sib.at[k, c], sibling)

    go_right(0, 0)
    go_left(0, 1)
    go_right(0, 1)
    go_left(0, 0)
    send(
        integ.at[:, :, pl.ds(pl.multiple_of(other * half, half), half)],
        wsib, w_sems.at[0], w_sems.at[1], sibling,
    )
    go_sib(0, 0)
    go_sib(0, 1)

    def put_w(j, w):
        hi = w.astype(BF16)
        wcat[j, :, :half] = hi
        wcat[j, :, half:] = (w - hi.astype(F32)).astype(BF16)

    @pl.loop(0, slots)
    def _(s):
        w = integ[s, :, pl.ds(pl.multiple_of(core * half, half), half)]
        put_w(s, w)

    got(wsib, w_sems.at[1], w_sems.at[0], sibling)

    @pl.loop(0, slots)
    def _(s):
        put_w(slots + s, wsib[s])

    def info(b, j):
        if j < slots:
            return meta[b, r * slots + j]
        return meta[b, sib_row * slots + j - slots]

    def compute(k):
        @pl.loop(0, blocks)
        def _(q):
            cols = pl.ds(pl.multiple_of(q * tile, tile), tile)
            for c in range(2):
                x = ag[k, c, :, cols]
                hi = x.astype(BF16)
                aw[q, c * rows:(c + 1) * rows, :] = hi
                aw[q, (2 + c) * rows:(3 + c) * rows, :] = (x - hi.astype(F32)).astype(BF16)

        for j in range(2 * slots):
            d = jnp.dot(aw[info(nt, j)], wcat[j], preferred_element_type=F32)
            top, low = d[:2 * rows], d[2 * rows:]
            prod[j] = (low[:, half:] + low[:, :half]) + top[:, half:] + top[:, :half]

        for b in range(nt):
            acc = None
            for j in range(2 * slots):
                term = prod[j] * info(b, j).astype(F32)
                acc = term if acc is None else acc + term
            for c in range(2):
                part[k, c, :, b * half:(b + 1) * half] = acc[c * rows:(c + 1) * rows]

    from_sib(0, 0)
    from_sib(0, 1)
    compute(0)

    for h in range(1, far):
        for c in range(2):
            cr, cl = c, 1 - c
            from_ring(h, cr)
            if h < far - 1 or cr == 0:
                go_right(h, cr)
            from_ring(n - h, cl)
            if h < far - 1 or cl == 1:
                go_left(n - h, cl)
            go_sib(h, cr)
            go_sib(n - h, cl)
        for k in (h, n - h):
            from_sib(k, 0)
            from_sib(k, 1)
            compute(k)

    def sum_right(k, c):
        send(part.at[k, c], rs.at[k + 1, c], rs_send.at[k, c, 0], rs_recv.at[k + 1, c], right)

    def sum_left(k, c):
        send(part.at[k, c], rs.at[k - 1, c], rs_send.at[k, c, 1], rs_recv.at[k - 1, c], left)

    def sum_got(k, c):
        got(rs.at[k, c], rs_recv.at[k, c], rs_send.at[k % n, c, 0], right)

    sum_right(far + 1, 1)
    sum_left(far - 1, 0)
    from_ring(far, 0)
    go_sib(far, 0)
    from_ring(far, 1)
    go_sib(far, 1)
    from_sib(far, 0)
    from_sib(far, 1)
    compute(far)
    sum_right(far, 0)
    sum_left(far, 1)

    def relay(k, c, onward):
        sum_got(k, c)
        if 0 < k < n:
            part[k, c] = part[k, c] + rs[k, c]
            onward(k, c)

    for t in range(1, far + 1):
        if far + 1 + t <= n:
            relay(far + 1 + t, 1, sum_right)
            relay(far - 1 - t, 0, sum_left)
        relay(far + t, 0, sum_right)
        relay(far - t, 1, sum_left)

    for c in range(2):
        part[0, c] = part[0, c] + rs[0, c] + rs[n, c]
    for c in range(2):
        send(
            part.at[0, c, pl.ds(pl.multiple_of(other * hr, hr), hr), :],
            fin.at[c], fin_sems.at[0, c], fin_sems.at[1, c], sibling,
        )
    for c in range(2):
        for b in range(nt):
            out[c * hr:(c + 1) * hr, pl.ds(pl.multiple_of(b * tile + core * half, half), half)] = (
                part[0, c, pl.ds(pl.multiple_of(core * hr, hr), hr), b * half:(b + 1) * half]
            )
    for c in range(2):
        got(fin.at[c], fin_sems.at[1, c], fin_sems.at[0, c], sibling)
        for b in range(nt):
            out[c * hr:(c + 1) * hr, pl.ds(pl.multiple_of(b * tile + other * half, half), half)] = (
                fin[c, :, b * half:(b + 1) * half]
            )
    for cp in pending:
        cp.wait_send()


def local(members, amps, amp_mask, integrals, slot_tile, int_mask):
    rows, width = amps.shape
    slots, tile, _ = integrals.shape
    nt = slot_tile.shape[0] // (width // tile)
    n = members // 2
    hr, half = rows // 2, tile // 2
    ids = jnp.arange(slot_tile.shape[0], dtype=jnp.int32)
    on = jnp.sum(jnp.where(slot_tile[None, :] == ids[:, None], int_mask[:, None], 0), axis=0)
    line = jnp.arange(nt + 1, dtype=jnp.int32)[:, None]
    meta = jnp.where(
        line < nt, jnp.where(slot_tile[None, :] % nt == line, on[None, :], 0), slot_tile[None, :] // nt
    )
    vmem = pl.BlockSpec(memory_space=pltpu.VMEM)
    smem = pl.BlockSpec(memory_space=pltpu.SMEM)
    dma = pltpu.SemaphoreType.DMA
    return pl.pallas_call(
        functools.partial(kernel, n, n == 8, nt),
        out_shape=jax.ShapeDtypeStruct((rows, nt * tile), F32),
        in_specs=[vmem, vmem, vmem, smem],
        out_specs=vmem,
        scratch_shapes=[
            pltpu.VMEM((n, 2, rows, width), F32),
            pltpu.VMEM((slots, tile, half), F32),
            pltpu.VMEM((2 * slots, tile, tile), BF16),
            pltpu.VMEM((width // tile, 4 * rows, tile), BF16),
            pltpu.VMEM((2 * slots, 2 * rows, half), F32),
            pltpu.VMEM((n, 2, rows, nt * half), F32),
            pltpu.VMEM((n + 1, 2, rows, nt * half), F32),
            pltpu.VMEM((2, hr, nt * half), F32),
            dma((n, 2, 2)),
            dma((n, 2)),
            dma((n, 2)),
            dma((n, 2)),
            dma((n + 1, 2)),
            dma((n, 2, 2)),
            dma((2,)),
            dma((2, 2)),
        ],
        compiler_params=pltpu.CompilerParams(
            collective_id=0, has_side_effects=True, vmem_limit_bytes=60 * 1024 * 1024
        ),
        cost_estimate=pl.CostEstimate(
            flops=8 * n * 2 * rows * slots * tile * tile,
            bytes_accessed=4 * (rows * width + slots * tile * tile + rows * nt * tile),
            transcendentals=0,
        ),
    )(amps, amp_mask, integrals, meta)


def solution(mesh):
    return jax.shard_map(
        functools.partial(local, mesh.shape["row"]),
        mesh=mesh,
        in_specs=(
            P(("grp", "row"), None),
            P("grp", None),
            P(("grp", "row"), None, None),
            P("grp"),
            P("grp"),
        ),
        out_specs=P(("grp", "row"), None),
        check_vma=False,
    )
```

```python
import functools

import jax
import jax.numpy as jnp
from jax import lax
from jax.experimental import pallas as pl
from jax.experimental.pallas import tpu as pltpu
from jax.sharding import PartitionSpec as P

PTILE = 4
MESH = pl.DeviceIdType.MESH
F32 = jnp.float32
BF16 = jnp.bfloat16


def kernel(
    n, snake, nt, amps, mask_t, integ, slot_tile, int_mask, out,
    ag, wown, wsib, gain_v, gain, block_v, block, wcat, aw, prod, part, rs, fin,
    ag_recv, ag_right, ag_left, ag_sib, rs_recv, rs_send, w_sems, fin_sems, own_sems,
):
    rows, width = amps.shape
    slots, tile, _ = integ.shape
    half = tile // 2
    blocks = width // tile
    hr = rows // 2
    far = n // 2
    grp = lax.axis_index("grp")
    r = lax.axis_index("row")
    chip, core = r // 2, r % 2
    other = 1 - core

    if snake:
        z, y, length = chip // 2, chip % 2, n // 2
        pos = (1 - y) * z + y * (n - 1 - z)

        def chip_at(q):
            up = q // length
            return (1 - up) * (2 * q) + up * (2 * (n - 1 - q) + 1)
    else:
        pos = chip

        def chip_at(q):
            return q

    right = (grp, chip_at((pos + 1) % n) * 2 + core)
    left = (grp, chip_at((pos + n - 1) % n) * 2 + core)
    sib_row = chip * 2 + other
    sibling = (grp, sib_row)

    barrier = pltpu.get_barrier_semaphore()
    for who in (right, left, sibling):
        pl.semaphore_signal(barrier, inc=1, device_id=who, device_id_type=MESH)

    def mine(k, c):
        return ag.at[k, c, pl.ds(pl.multiple_of(core * hr, hr), hr), :]

    own_w = pltpu.make_async_copy(
        integ.at[:, :, pl.ds(pl.multiple_of(core * half, half), half)], wown, own_sems.at[0]
    )
    own_w.start()

    mrows = mask_t.shape[1]
    shape = (rows, mrows)
    pick = (
        lax.broadcasted_iota(jnp.int32, shape, 1)
        == lax.broadcasted_iota(jnp.int32, shape, 0) // PTILE + r * (rows // PTILE)
    ).astype(F32)
    mask = lax.dot_general(
        pick, mask_t[...].astype(F32), (((1,), (1,)), ((), ())), preferred_element_type=F32
    )
    for j in range(blocks):
        seg = amps[:, j * tile:(j + 1) * tile] * mask[:, j:j + 1]
        for c in range(2):
            ag[0, c, pl.ds(pl.multiple_of(core * hr, hr), hr), j * tile:(j + 1) * tile] = (
                seg[c * hr:(c + 1) * hr]
            )

    pl.semaphore_wait(barrier, 3)

    pending = []

    def send(src, dst, ssem, rsem, who):
        cp = pltpu.make_async_remote_copy(
            src_ref=src, dst_ref=dst, send_sem=ssem, recv_sem=rsem,
            device_id=who, device_id_type=MESH,
        )
        cp.start()
        pending.append(cp)

    def got(dst, rsem, ssem, who):
        pltpu.make_async_remote_copy(
            src_ref=dst, dst_ref=dst, send_sem=ssem, recv_sem=rsem,
            device_id=who, device_id_type=MESH,
        ).wait_recv()

    def go_right(k, c):
        send(mine(k, c), mine(k + 1, c), ag_right.at[k, c], ag_recv.at[k + 1, c, 0], right)

    def go_left(k, c):
        k0 = k if k else n
        send(mine(k, c), mine(k0 - 1, c), ag_left.at[k, c], ag_recv.at[k0 - 1, c, 0], left)

    def go_sib(k, c):
        send(mine(k, c), mine(k, c), ag_sib.at[k, c], ag_recv.at[k, c, 1], sibling)

    def from_ring(k, c):
        got(mine(k, c), ag_recv.at[k, c, 0], ag_sib.at[k, c], sibling)

    def from_sib(k, c):
        theirs = ag.at[k, c, pl.ds(pl.multiple_of(other * hr, hr), hr), :]
        got(theirs, ag_recv.at[k, c, 1], ag_sib.at[k, c], sibling)

    go_right(0, 0)
    go_left(0, 1)
    go_right(0, 1)
    go_left(0, 0)
    send(
        integ.at[:, :, pl.ds(pl.multiple_of(other * half, half), half)],
        wsib, w_sems.at[0], w_sems.at[1], sibling,
    )
    go_sib(0, 0)
    go_sib(0, 1)

    count = slot_tile.shape[1]
    tiles = jnp.broadcast_to(slot_tile[...], (count, count))
    hot = (tiles == lax.broadcasted_iota(jnp.int32, (count, count), 0)).astype(F32)
    on = jnp.dot(int_mask[...].astype(F32), hot, preferred_element_type=F32)
    tiles = jnp.broadcast_to(slot_tile[...], (nt, count))
    here = (tiles % nt == lax.broadcasted_iota(jnp.int32, (nt, count), 0)).astype(F32)
    gain_v[...] = here * on
    block_v[...] = tiles // nt
    tables = (
        pltpu.make_async_copy(gain_v, gain, own_sems.at[1]),
        pltpu.make_async_copy(block_v, block, own_sems.at[2]),
    )
    for cp in tables:
        cp.start()

    def put_w(j, w):
        hi = w.astype(BF16)
        wcat[j, :, :half] = hi
        wcat[j, :, half:] = (w - hi.astype(F32)).astype(BF16)

    own_w.wait()

    @pl.loop(0, slots)
    def _(s):
        put_w(s, wown[s])

    got(wsib, w_sems.at[1], w_sems.at[0], sibling)

    @pl.loop(0, slots)
    def _(s):
        put_w(slots + s, wsib[s])

    for cp in tables:
        cp.wait()

    def slot_of(j):
        return r * slots + j if j < slots else sib_row * slots + j - slots

    def compute(k):
        @pl.loop(0, blocks)
        def _(q):
            cols = pl.ds(pl.multiple_of(q * tile, tile), tile)
            for c in range(2):
                x = ag[k, c, :, cols]
                hi = x.astype(BF16)
                aw[q, c * rows:(c + 1) * rows, :] = hi
                aw[q, (2 + c) * rows:(3 + c) * rows, :] = (x - hi.astype(F32)).astype(BF16)

        for j in range(2 * slots):
            d = jnp.dot(aw[block[0, slot_of(j)]], wcat[j], preferred_element_type=F32)
            top, low = d[:2 * rows], d[2 * rows:]
            prod[j] = (low[:, half:] + low[:, :half]) + top[:, half:] + top[:, :half]

        for b in range(nt):
            acc = None
            for j in range(2 * slots):
                term = prod[j] * gain[b, slot_of(j)]
                acc = term if acc is None else acc + term
            for c in range(2):
                part[k, c, :, b * half:(b + 1) * half] = acc[c * rows:(c + 1) * rows]

    from_sib(0, 0)
    from_sib(0, 1)
    compute(0)

    for h in range(1, far):
        for c in range(2):
            cr, cl = c, 1 - c
            from_ring(h, cr)
            if h < far - 1 or cr == 0:
                go_right(h, cr)
            from_ring(n - h, cl)
            if h < far - 1 or cl == 1:
                go_left(n - h, cl)
            go_sib(h, cr)
            go_sib(n - h, cl)
        for k in (h, n - h):
            from_sib(k, 0)
            from_sib(k, 1)
            compute(k)

    def sum_right(k, c):
        send(part.at[k, c], rs.at[k + 1, c], rs_send.at[k, c, 0], rs_recv.at[k + 1, c], right)

    def sum_left(k, c):
        send(part.at[k, c], rs.at[k - 1, c], rs_send.at[k, c, 1], rs_recv.at[k - 1, c], left)

    def sum_got(k, c):
        got(rs.at[k, c], rs_recv.at[k, c], rs_send.at[k % n, c, 0], right)

    sum_right(far + 1, 1)
    sum_left(far - 1, 0)
    from_ring(far, 0)
    go_sib(far, 0)
    from_ring(far, 1)
    go_sib(far, 1)
    from_sib(far, 0)
    from_sib(far, 1)
    compute(far)
    sum_right(far, 0)
    sum_left(far, 1)

    def relay(k, c, onward):
        sum_got(k, c)
        if 0 < k < n:
            part[k, c] = part[k, c] + rs[k, c]
            onward(k, c)

    for t in range(1, far + 1):
        if far + 1 + t <= n:
            relay(far + 1 + t, 1, sum_right)
            relay(far - 1 - t, 0, sum_left)
        relay(far + t, 0, sum_right)
        relay(far - t, 1, sum_left)

    for c in range(2):
        part[0, c] = part[0, c] + rs[0, c] + rs[n, c]
    for c in range(2):
        send(
            part.at[0, c, pl.ds(pl.multiple_of(other * hr, hr), hr), :],
            fin.at[c], fin_sems.at[0, c], fin_sems.at[1, c], sibling,
        )
    for c in range(2):
        for b in range(nt):
            out[c * hr:(c + 1) * hr, pl.ds(pl.multiple_of(b * tile + core * half, half), half)] = (
                part[0, c, pl.ds(pl.multiple_of(core * hr, hr), hr), b * half:(b + 1) * half]
            )
    for c in range(2):
        got(fin.at[c], fin_sems.at[1, c], fin_sems.at[0, c], sibling)
        for b in range(nt):
            out[c * hr:(c + 1) * hr, pl.ds(pl.multiple_of(b * tile + other * half, half), half)] = (
                fin[c, :, b * half:(b + 1) * half]
            )
    for cp in pending:
        cp.wait_send()


def local(members, amps, amp_mask, integrals, slot_tile, int_mask):
    rows, width = amps.shape
    slots, tile, _ = integrals.shape
    nt = slot_tile.shape[0] // (width // tile)
    n = members // 2
    hr, half = rows // 2, tile // 2
    vmem = pl.BlockSpec(memory_space=pltpu.VMEM)
    count = slot_tile.shape[0]
    dma = pltpu.SemaphoreType.DMA
    return pl.pallas_call(
        functools.partial(kernel, n, n == 8, nt),
        out_shape=jax.ShapeDtypeStruct((rows, nt * tile), F32),
        in_specs=[vmem, vmem, pl.BlockSpec(memory_space=pl.ANY), vmem, vmem],
        out_specs=vmem,
        scratch_shapes=[
            pltpu.VMEM((n, 2, rows, width), F32),
            pltpu.VMEM((slots, tile, half), F32),
            pltpu.VMEM((slots, tile, half), F32),
            pltpu.VMEM((nt, count), F32),
            pltpu.SMEM((nt, count), F32),
            pltpu.VMEM((nt, count), jnp.int32),
            pltpu.SMEM((nt, count), jnp.int32),
            pltpu.VMEM((2 * slots, tile, tile), BF16),
            pltpu.VMEM((width // tile, 4 * rows, tile), BF16),
            pltpu.VMEM((2 * slots, 2 * rows, half), F32),
            pltpu.VMEM((n, 2, rows, nt * half), F32),
            pltpu.VMEM((n + 1, 2, rows, nt * half), F32),
            pltpu.VMEM((2, hr, nt * half), F32),
            dma((n, 2, 2)),
            dma((n, 2)),
            dma((n, 2)),
            dma((n, 2)),
            dma((n + 1, 2)),
            dma((n, 2, 2)),
            dma((2,)),
            dma((2, 2)),
            dma((3,)),
        ],
        compiler_params=pltpu.CompilerParams(
            collective_id=0, has_side_effects=True, vmem_limit_bytes=60 * 1024 * 1024
        ),
        cost_estimate=pl.CostEstimate(
            flops=8 * n * 2 * rows * slots * tile * tile,
            bytes_accessed=4 * (rows * width + slots * tile * tile + rows * nt * tile),
            transcendentals=0,
        ),
    )(amps, amp_mask.T, integrals, slot_tile.reshape(1, count), int_mask.reshape(1, count))


def solution(mesh):
    return jax.shard_map(
        functools.partial(local, mesh.shape["row"]),
        mesh=mesh,
        in_specs=(
            P(("grp", "row"), None),
            P("grp", None),
            P(("grp", "row"), None, None),
            P("grp"),
            P("grp"),
        ),
        out_specs=P(("grp", "row"), None),
        check_vma=False,
    )
```

```python
import functools

import jax
import jax.numpy as jnp
from jax import lax
from jax.experimental import pallas as pl
from jax.experimental.pallas import tpu as pltpu
from jax.sharding import PartitionSpec as P

PTILE = 4
MESH = pl.DeviceIdType.MESH
F32 = jnp.float32
BF16 = jnp.bfloat16


def kernel(
    n, snake, nt, amps, mask_t, integ, slot_tile, int_mask, out,
    ag, wown, wsib, gain_v, gain, block_v, block, wcat, aw, prod, part, rs, last, fin,
    ag_recv, ag_right, ag_left, ag_sib, rs_recv, rs_send, w_sems, fin_sems, own_sems, last_recv, last_send,
):
    rows, width = amps.shape
    slots, tile, _ = integ.shape
    half = tile // 2
    blocks = width // tile
    hr = rows // 2
    far = n // 2
    grp = lax.axis_index("grp")
    r = lax.axis_index("row")
    chip, core = r // 2, r % 2
    other = 1 - core

    if snake:
        z, y, length = chip // 2, chip % 2, n // 2
        pos = (1 - y) * z + y * (n - 1 - z)

        def chip_at(q):
            up = q // length
            return (1 - up) * (2 * q) + up * (2 * (n - 1 - q) + 1)
    else:
        pos = chip

        def chip_at(q):
            return q

    right_chip, left_chip = chip_at((pos + 1) % n), chip_at((pos + n - 1) % n)
    right, right_other = (grp, right_chip * 2 + core), (grp, right_chip * 2 + other)
    left, left_other = (grp, left_chip * 2 + core), (grp, left_chip * 2 + other)
    sib_row = chip * 2 + other
    sibling = (grp, sib_row)

    barrier = pltpu.get_barrier_semaphore()
    for who in (right, left, right_other, left_other, sibling):
        pl.semaphore_signal(barrier, inc=1, device_id=who, device_id_type=MESH)

    def mine(k, c):
        return ag.at[k, c, pl.ds(pl.multiple_of(core * hr, hr), hr), :]

    own_w = pltpu.make_async_copy(
        integ.at[:, :, pl.ds(pl.multiple_of(core * half, half), half)], wown, own_sems.at[0]
    )
    own_w.start()

    mrows = mask_t.shape[1]
    shape = (rows, mrows)
    pick = (
        lax.broadcasted_iota(jnp.int32, shape, 1)
        == lax.broadcasted_iota(jnp.int32, shape, 0) // PTILE + r * (rows // PTILE)
    ).astype(F32)
    mask = lax.dot_general(
        pick, mask_t[...].astype(F32), (((1,), (1,)), ((), ())), preferred_element_type=F32
    )
    for j in range(blocks):
        seg = amps[:, j * tile:(j + 1) * tile] * mask[:, j:j + 1]
        for c in range(2):
            ag[0, c, pl.ds(pl.multiple_of(core * hr, hr), hr), j * tile:(j + 1) * tile] = (
                seg[c * hr:(c + 1) * hr]
            )

    pl.semaphore_wait(barrier, 5)

    pending = []

    def send(src, dst, ssem, rsem, who):
        cp = pltpu.make_async_remote_copy(
            src_ref=src, dst_ref=dst, send_sem=ssem, recv_sem=rsem,
            device_id=who, device_id_type=MESH,
        )
        cp.start()
        pending.append(cp)

    def got(dst, rsem, ssem, who):
        pltpu.make_async_remote_copy(
            src_ref=dst, dst_ref=dst, send_sem=ssem, recv_sem=rsem,
            device_id=who, device_id_type=MESH,
        ).wait_recv()

    def go_right(k, c):
        send(mine(k, c), mine(k + 1, c), ag_right.at[k, c], ag_recv.at[k + 1, c, 0], right)

    def go_left(k, c):
        k0 = k if k else n
        send(mine(k, c), mine(k0 - 1, c), ag_left.at[k, c], ag_recv.at[k0 - 1, c, 0], left)

    def go_sib(k, c):
        send(mine(k, c), mine(k, c), ag_sib.at[k, c], ag_recv.at[k, c, 1], sibling)

    def from_ring(k, c):
        got(mine(k, c), ag_recv.at[k, c, 0], ag_sib.at[k, c], sibling)

    def from_sib(k, c):
        rest = ag.at[k, c, pl.ds(pl.multiple_of(other * hr, hr), hr), :]
        got(rest, ag_recv.at[k, c, 1], ag_sib.at[k, c], sibling)

    go_right(0, 0)
    go_left(0, 1)
    go_right(0, 1)
    go_left(0, 0)
    send(
        integ.at[:, :, pl.ds(pl.multiple_of(other * half, half), half)],
        wsib, w_sems.at[0], w_sems.at[1], sibling,
    )
    go_sib(0, 0)
    go_sib(0, 1)

    count = slot_tile.shape[1]
    tiles = jnp.broadcast_to(slot_tile[...], (count, count))
    hot = (tiles == lax.broadcasted_iota(jnp.int32, (count, count), 0)).astype(F32)
    on = jnp.dot(int_mask[...].astype(F32), hot, preferred_element_type=F32)
    tiles = jnp.broadcast_to(slot_tile[...], (nt, count))
    here = (tiles % nt == lax.broadcasted_iota(jnp.int32, (nt, count), 0)).astype(F32)
    gain_v[...] = here * on
    block_v[...] = tiles // nt
    tables = (
        pltpu.make_async_copy(gain_v, gain, own_sems.at[1]),
        pltpu.make_async_copy(block_v, block, own_sems.at[2]),
    )
    for cp in tables:
        cp.start()

    def put_w(j, w):
        hi = w.astype(BF16)
        wcat[j, :, :half] = hi
        wcat[j, :, half:] = (w - hi.astype(F32)).astype(BF16)

    own_w.wait()

    @pl.loop(0, slots)
    def _(s):
        put_w(s, wown[s])

    got(wsib, w_sems.at[1], w_sems.at[0], sibling)

    @pl.loop(0, slots)
    def _(s):
        put_w(slots + s, wsib[s])

    for cp in tables:
        cp.wait()

    def slot_of(j):
        return r * slots + j if j < slots else sib_row * slots + j - slots

    def compute(k):
        @pl.loop(0, blocks)
        def _(q):
            cols = pl.ds(pl.multiple_of(q * tile, tile), tile)
            for c in range(2):
                x = ag[k, c, :, cols]
                hi = x.astype(BF16)
                aw[q, c * rows:(c + 1) * rows, :] = hi
                aw[q, (2 + c) * rows:(3 + c) * rows, :] = (x - hi.astype(F32)).astype(BF16)

        for j in range(2 * slots):
            d = jnp.dot(aw[block[0, slot_of(j)]], wcat[j], preferred_element_type=F32)
            top, low = d[:2 * rows], d[2 * rows:]
            prod[j] = (low[:, half:] + low[:, :half]) + top[:, half:] + top[:, :half]

        for b in range(nt):
            acc = None
            for j in range(2 * slots):
                term = prod[j] * gain[b, slot_of(j)]
                acc = term if acc is None else acc + term
            for c in range(2):
                part[k, c, :, b * half:(b + 1) * half] = acc[c * rows:(c + 1) * rows]

    from_sib(0, 0)
    from_sib(0, 1)
    compute(0)
    own = pl.ds(pl.multiple_of(core * hr, hr), hr)
    theirs = pl.ds(pl.multiple_of(other * hr, hr), hr)
    for c in range(2):
        send(
            part.at[0, c, theirs, :], fin.at[c], fin_sems.at[0, c], fin_sems.at[1, c], sibling
        )

    for h in range(1, far):
        for c in range(2):
            cr, cl = c, 1 - c
            from_ring(h, cr)
            if h < far - 1 or cr == 0:
                go_right(h, cr)
            from_ring(n - h, cl)
            if h < far - 1 or cl == 1:
                go_left(n - h, cl)
            go_sib(h, cr)
            go_sib(n - h, cl)
        for k in (h, n - h):
            from_sib(k, 0)
            from_sib(k, 1)
            compute(k)

    def deliver(k, c, way, same, cross):
        send(
            part.at[k, c, own, :], last.at[way, c, core],
            rs_send.at[k, c, way], last_recv.at[way, c, core], same,
        )
        send(
            part.at[k, c, theirs, :], last.at[way, c, core],
            last_send.at[way, c], last_recv.at[way, c, core], cross,
        )

    def sum_right(k, c):
        if k + 1 == n:
            return deliver(k, c, 0, right, right_other)
        send(part.at[k, c], rs.at[k + 1, c], rs_send.at[k, c, 0], rs_recv.at[k + 1, c], right)

    def sum_left(k, c):
        if k == 1:
            return deliver(k, c, 1, left, left_other)
        send(part.at[k, c], rs.at[k - 1, c], rs_send.at[k, c, 1], rs_recv.at[k - 1, c], left)

    sum_right(far + 1, 1)
    sum_left(far - 1, 0)
    from_ring(far, 0)
    go_sib(far, 0)
    from_ring(far, 1)
    go_sib(far, 1)

    def relay(k, c, onward):
        if 0 < k < n:
            got(rs.at[k, c], rs_recv.at[k, c], rs_send.at[k, c, 0], right)
            part[k, c] = part[k, c] + rs[k, c]
            onward(k, c)

    from_sib(far, 0)
    from_sib(far, 1)
    compute(far)
    sum_right(far, 0)
    sum_left(far, 1)
    for t in range(1, far):
        relay(far + 1 + t, 1, sum_right)
        relay(far - 1 - t, 0, sum_left)
        relay(far + t, 0, sum_right)
        relay(far - t, 1, sum_left)

    for c in range(2):
        got(fin.at[c], fin_sems.at[1, c], fin_sems.at[0, c], sibling)
    for c in range(2):
        for way in ((0, 1) if c else (1, 0)):
            for q in range(2):
                got(last.at[way, c, q], last_recv.at[way, c, q], last_send.at[way, c], right)
        for src, q in ((part.at[0, c, own, :], core), (fin.at[c], other)):
            for b in range(nt):
                cols = slice(b * half, (b + 1) * half)
                out[c * hr:(c + 1) * hr, pl.ds(pl.multiple_of(b * tile + q * half, half), half)] = (
                    src[:, cols] + last[0, c, q, :, cols] + last[1, c, q, :, cols]
                )
    for cp in pending:
        cp.wait_send()


def local(members, amps, amp_mask, integrals, slot_tile, int_mask):
    rows, width = amps.shape
    slots, tile, _ = integrals.shape
    nt = slot_tile.shape[0] // (width // tile)
    n = members // 2
    hr, half = rows // 2, tile // 2
    vmem = pl.BlockSpec(memory_space=pltpu.VMEM)
    count = slot_tile.shape[0]
    dma = pltpu.SemaphoreType.DMA
    return pl.pallas_call(
        functools.partial(kernel, n, n == 8, nt),
        out_shape=jax.ShapeDtypeStruct((rows, nt * tile), F32),
        in_specs=[vmem, vmem, pl.BlockSpec(memory_space=pl.ANY), vmem, vmem],
        out_specs=vmem,
        scratch_shapes=[
            pltpu.VMEM((n, 2, rows, width), F32),
            pltpu.VMEM((slots, tile, half), F32),
            pltpu.VMEM((slots, tile, half), F32),
            pltpu.VMEM((nt, count), F32),
            pltpu.SMEM((nt, count), F32),
            pltpu.VMEM((nt, count), jnp.int32),
            pltpu.SMEM((nt, count), jnp.int32),
            pltpu.VMEM((2 * slots, tile, tile), BF16),
            pltpu.VMEM((width // tile, 4 * rows, tile), BF16),
            pltpu.VMEM((2 * slots, 2 * rows, half), F32),
            pltpu.VMEM((n, 2, rows, nt * half), F32),
            pltpu.VMEM((n, 2, rows, nt * half), F32),
            pltpu.VMEM((2, 2, 2, hr, nt * half), F32),
            pltpu.VMEM((2, hr, nt * half), F32),
            dma((n, 2, 2)),
            dma((n, 2)),
            dma((n, 2)),
            dma((n, 2)),
            dma((n, 2)),
            dma((n, 2, 2)),
            dma((2,)),
            dma((2, 2)),
            dma((3,)),
            dma((2, 2, 2)),
            dma((2, 2)),
        ],
        compiler_params=pltpu.CompilerParams(
            collective_id=0, has_side_effects=True, vmem_limit_bytes=60 * 1024 * 1024
        ),
        cost_estimate=pl.CostEstimate(
            flops=8 * n * 2 * rows * slots * tile * tile,
            bytes_accessed=4 * (rows * width + slots * tile * tile + rows * nt * tile),
            transcendentals=0,
        ),
    )(amps, amp_mask.T, integrals, slot_tile.reshape(1, count), int_mask.reshape(1, count))


def solution(mesh):
    return jax.shard_map(
        functools.partial(local, mesh.shape["row"]),
        mesh=mesh,
        in_specs=(
            P(("grp", "row"), None),
            P("grp", None),
            P(("grp", "row"), None, None),
            P("grp"),
            P("grp"),
        ),
        out_specs=P(("grp", "row"), None),
        check_vma=False,
    )
```

```python
import functools

import jax
import jax.numpy as jnp
from jax import lax
from jax.experimental import pallas as pl
from jax.experimental.pallas import tpu as pltpu
from jax.sharding import PartitionSpec as P

PTILE = 4
MESH = pl.DeviceIdType.MESH
F32 = jnp.float32
BF16 = jnp.bfloat16


def kernel(
    n, snake, nt, amps, mask_t, integ, slot_tile, int_mask, out,
    ag, wown, wsib, gain_v, gain, block_v, block, wcat, aw, prod, part, rs, last, fin,
    ag_recv, ag_right, ag_left, ag_sib, rs_recv, rs_send, w_sems, fin_sems, own_sems, last_recv, last_send,
):
    rows, width = amps.shape
    slots, tile, _ = integ.shape
    half = tile // 2
    blocks = width // tile
    hr = rows // 2
    far = n // 2
    grp = lax.axis_index("grp")
    r = lax.axis_index("row")
    chip, core = r // 2, r % 2
    other = 1 - core

    if snake:
        z, y, length = chip // 2, chip % 2, n // 2
        pos = (1 - y) * z + y * (n - 1 - z)

        def chip_at(q):
            up = q // length
            return (1 - up) * (2 * q) + up * (2 * (n - 1 - q) + 1)
    else:
        pos = chip

        def chip_at(q):
            return q

    right_chip, left_chip = chip_at((pos + 1) % n), chip_at((pos + n - 1) % n)
    right, right_other = (grp, right_chip * 2 + core), (grp, right_chip * 2 + other)
    left, left_other = (grp, left_chip * 2 + core), (grp, left_chip * 2 + other)
    sib_row = chip * 2 + other
    sibling = (grp, sib_row)

    barrier = pltpu.get_barrier_semaphore()
    for who in (right, left, right_other, left_other, sibling):
        pl.semaphore_signal(barrier, inc=1, device_id=who, device_id_type=MESH)

    def mine(k, c):
        return ag.at[k, c, pl.ds(pl.multiple_of(core * hr, hr), hr), :]

    own_w = pltpu.make_async_copy(
        integ.at[:, :, pl.ds(pl.multiple_of(core * half, half), half)], wown, own_sems.at[0]
    )
    own_w.start()

    mrows = mask_t.shape[1]
    shape = (rows, mrows)
    pick = (
        lax.broadcasted_iota(jnp.int32, shape, 1)
        == lax.broadcasted_iota(jnp.int32, shape, 0) // PTILE + r * (rows // PTILE)
    ).astype(F32)
    mask = lax.dot_general(
        pick, mask_t[...].astype(F32), (((1,), (1,)), ((), ())), preferred_element_type=F32
    )
    for j in range(blocks):
        seg = amps[:, j * tile:(j + 1) * tile] * mask[:, j:j + 1]
        for c in range(2):
            ag[0, c, pl.ds(pl.multiple_of(core * hr, hr), hr), j * tile:(j + 1) * tile] = (
                seg[c * hr:(c + 1) * hr]
            )

    pl.semaphore_wait(barrier, 5)

    pending = []

    def send(src, dst, ssem, rsem, who):
        cp = pltpu.make_async_remote_copy(
            src_ref=src, dst_ref=dst, send_sem=ssem, recv_sem=rsem,
            device_id=who, device_id_type=MESH,
        )
        cp.start()
        pending.append(cp)

    def got(dst, rsem, ssem, who):
        pltpu.make_async_remote_copy(
            src_ref=dst, dst_ref=dst, send_sem=ssem, recv_sem=rsem,
            device_id=who, device_id_type=MESH,
        ).wait_recv()

    def go_right(k, c):
        send(mine(k, c), mine(k + 1, c), ag_right.at[k, c], ag_recv.at[k + 1, c, 0], right)

    def go_left(k, c):
        k0 = k if k else n
        send(mine(k, c), mine(k0 - 1, c), ag_left.at[k, c], ag_recv.at[k0 - 1, c, 0], left)

    def go_sib(k, c):
        send(mine(k, c), mine(k, c), ag_sib.at[k, c], ag_recv.at[k, c, 1], sibling)

    def from_ring(k, c):
        got(mine(k, c), ag_recv.at[k, c, 0], ag_sib.at[k, c], sibling)

    def from_sib(k, c):
        rest = ag.at[k, c, pl.ds(pl.multiple_of(other * hr, hr), hr), :]
        got(rest, ag_recv.at[k, c, 1], ag_sib.at[k, c], sibling)

    go_right(0, 0)
    go_left(0, 1)
    go_right(0, 1)
    go_left(0, 0)
    send(
        integ.at[:, :, pl.ds(pl.multiple_of(other * half, half), half)],
        wsib, w_sems.at[0], w_sems.at[1], sibling,
    )
    go_sib(0, 0)
    go_sib(0, 1)

    count = slot_tile.shape[1]
    tiles = jnp.broadcast_to(slot_tile[...], (count, count))
    hot = (tiles == lax.broadcasted_iota(jnp.int32, (count, count), 0)).astype(F32)
    on = jnp.dot(int_mask[...].astype(F32), hot, preferred_element_type=F32)
    tiles = jnp.broadcast_to(slot_tile[...], (nt, count))
    here = (tiles % nt == lax.broadcasted_iota(jnp.int32, (nt, count), 0)).astype(F32)
    gain_v[...] = here * on
    block_v[...] = tiles // nt
    tables = (
        pltpu.make_async_copy(gain_v, gain, own_sems.at[1]),
        pltpu.make_async_copy(block_v, block, own_sems.at[2]),
    )
    for cp in tables:
        cp.start()

    def put_w(j, w):
        hi = w.astype(BF16)
        wcat[j, :, :half] = hi
        wcat[j, :, half:] = (w - hi.astype(F32)).astype(BF16)

    own_w.wait()

    @pl.loop(0, slots)
    def _(s):
        put_w(s, wown[s])

    got(wsib, w_sems.at[1], w_sems.at[0], sibling)

    @pl.loop(0, slots)
    def _(s):
        put_w(slots + s, wsib[s])

    for cp in tables:
        cp.wait()

    def slot_of(j):
        return r * slots + j if j < slots else sib_row * slots + j - slots

    def compute(k):
        @pl.loop(0, blocks)
        def _(q):
            cols = pl.ds(pl.multiple_of(q * tile, tile), tile)
            for c in range(2):
                x = ag[k, c, :, cols]
                hi = x.astype(BF16)
                aw[q, c * rows:(c + 1) * rows, :] = hi
                aw[q, (2 + c) * rows:(3 + c) * rows, :] = (x - hi.astype(F32)).astype(BF16)

        for j in range(2 * slots):
            d = jnp.dot(aw[block[0, slot_of(j)]], wcat[j], preferred_element_type=F32)
            top, low = d[:2 * rows], d[2 * rows:]
            prod[j] = (low[:, half:] + low[:, :half]) + top[:, half:] + top[:, :half]

        for b in range(nt):
            acc = None
            for j in range(2 * slots):
                term = prod[j] * gain[b, slot_of(j)]
                acc = term if acc is None else acc + term
            for c in range(2):
                part[k, c, :, b * half:(b + 1) * half] = acc[c * rows:(c + 1) * rows]

    from_sib(0, 0)
    from_sib(0, 1)
    compute(0)
    own = pl.ds(pl.multiple_of(core * hr, hr), hr)
    theirs = pl.ds(pl.multiple_of(other * hr, hr), hr)
    for c in range(2):
        send(
            part.at[0, c, theirs, :], fin.at[c], fin_sems.at[0, c], fin_sems.at[1, c], sibling
        )

    for h in range(1, far):
        for c in range(2):
            cr, cl = c, 1 - c
            from_ring(h, cr)
            if h < far - 1 or cr == 0:
                go_right(h, cr)
            from_ring(n - h, cl)
            if h < far - 1 or cl == 1:
                go_left(n - h, cl)
            go_sib(h, cr)
            go_sib(n - h, cl)
        for k in (h, n - h):
            from_sib(k, 0)
            from_sib(k, 1)
            compute(k)

    def deliver(k, c, way, same, cross):
        send(
            part.at[k, c, own, :], last.at[way, c, core],
            rs_send.at[k, c, way], last_recv.at[way, c, core], same,
        )
        send(
            part.at[k, c, theirs, :], last.at[way, c, core],
            last_send.at[way, c], last_recv.at[way, c, core], cross,
        )

    def sum_right(k, c):
        if k + 1 == n:
            return deliver(k, c, 0, right, right_other)
        send(part.at[k, c], rs.at[k + 1, c], rs_send.at[k, c, 0], rs_recv.at[k + 1, c], right)

    def sum_left(k, c):
        if k == 1:
            return deliver(k, c, 1, left, left_other)
        send(part.at[k, c], rs.at[k - 1, c], rs_send.at[k, c, 1], rs_recv.at[k - 1, c], left)

    sum_right(far + 1, 1)
    sum_left(far - 1, 0)
    from_ring(far, 0)
    go_sib(far, 0)
    from_ring(far, 1)
    go_sib(far, 1)

    def relay(k, c, onward):
        if 0 < k < n:
            got(rs.at[k, c], rs_recv.at[k, c], rs_send.at[k, c, 0], right)
            part[k, c] = part[k, c] + rs[k, c]
            onward(k, c)

    relay(far + 2, 1, sum_right)
    relay(far - 2, 0, sum_left)
    from_sib(far, 0)
    from_sib(far, 1)
    compute(far)
    sum_right(far, 0)
    sum_left(far, 1)
    for t in range(1, far):
        relay(far + 2 + t, 1, sum_right)
        relay(far - 2 - t, 0, sum_left)
        relay(far + t, 0, sum_right)
        relay(far - t, 1, sum_left)

    for c in range(2):
        got(fin.at[c], fin_sems.at[1, c], fin_sems.at[0, c], sibling)
    for c in range(2):
        for way in ((0, 1) if c else (1, 0)):
            for q in range(2):
                got(last.at[way, c, q], last_recv.at[way, c, q], last_send.at[way, c], right)
        for src, q in ((part.at[0, c, own, :], core), (fin.at[c], other)):
            for b in range(nt):
                cols = slice(b * half, (b + 1) * half)
                out[c * hr:(c + 1) * hr, pl.ds(pl.multiple_of(b * tile + q * half, half), half)] = (
                    src[:, cols] + last[0, c, q, :, cols] + last[1, c, q, :, cols]
                )
    for cp in pending:
        cp.wait_send()


def local(members, amps, amp_mask, integrals, slot_tile, int_mask):
    rows, width = amps.shape
    slots, tile, _ = integrals.shape
    nt = slot_tile.shape[0] // (width // tile)
    n = members // 2
    hr, half = rows // 2, tile // 2
    vmem = pl.BlockSpec(memory_space=pltpu.VMEM)
    count = slot_tile.shape[0]
    dma = pltpu.SemaphoreType.DMA
    return pl.pallas_call(
        functools.partial(kernel, n, n == 8, nt),
        out_shape=jax.ShapeDtypeStruct((rows, nt * tile), F32),
        in_specs=[vmem, vmem, pl.BlockSpec(memory_space=pl.ANY), vmem, vmem],
        out_specs=vmem,
        scratch_shapes=[
            pltpu.VMEM((n, 2, rows, width), F32),
            pltpu.VMEM((slots, tile, half), F32),
            pltpu.VMEM((slots, tile, half), F32),
            pltpu.VMEM((nt, count), F32),
            pltpu.SMEM((nt, count), F32),
            pltpu.VMEM((nt, count), jnp.int32),
            pltpu.SMEM((nt, count), jnp.int32),
            pltpu.VMEM((2 * slots, tile, tile), BF16),
            pltpu.VMEM((width // tile, 4 * rows, tile), BF16),
            pltpu.VMEM((2 * slots, 2 * rows, half), F32),
            pltpu.VMEM((n, 2, rows, nt * half), F32),
            pltpu.VMEM((n, 2, rows, nt * half), F32),
            pltpu.VMEM((2, 2, 2, hr, nt * half), F32),
            pltpu.VMEM((2, hr, nt * half), F32),
            dma((n, 2, 2)),
            dma((n, 2)),
            dma((n, 2)),
            dma((n, 2)),
            dma((n, 2)),
            dma((n, 2, 2)),
            dma((2,)),
            dma((2, 2)),
            dma((3,)),
            dma((2, 2, 2)),
            dma((2, 2)),
        ],
        compiler_params=pltpu.CompilerParams(
            collective_id=0, has_side_effects=True, vmem_limit_bytes=60 * 1024 * 1024
        ),
        cost_estimate=pl.CostEstimate(
            flops=8 * n * 2 * rows * slots * tile * tile,
            bytes_accessed=4 * (rows * width + slots * tile * tile + rows * nt * tile),
            transcendentals=0,
        ),
    )(amps, amp_mask.T, integrals, slot_tile.reshape(1, count), int_mask.reshape(1, count))


def solution(mesh):
    return jax.shard_map(
        functools.partial(local, mesh.shape["row"]),
        mesh=mesh,
        in_specs=(
            P(("grp", "row"), None),
            P("grp", None),
            P(("grp", "row"), None, None),
            P("grp"),
            P("grp"),
        ),
        out_specs=P(("grp", "row"), None),
        check_vma=False,
    )
```
